32 devices in a mesh: temp: 2 (over y), row: 4 (over x, core), col: 4 (over z).
Axes of the slice: x: 2, y: 2, z: 4, core: 2. Of those that a mesh axis runs over, the one named last changes fastest.
Arguments:
- subspace: bfloat16 [32768, 128], P(('temp', 'row', 'col')), parts along dimension 0, may hold values from -6 to 6
- hamiltonian: bfloat16 [768, 512, 512], P(('temp', 'row', 'col')), parts along dimension 0
- tile_blocks: int32 [16, 24, 2], P(('row', 'col')), may hold values from 0 to 31, as said below
- tile_count: int32 [16], P(('row', 'col')), may hold values from 2 to 24, as said below
- cut_bound: float32 [2], P('temp'), parts along dimension 0, may hold values from -0.6 to 0.2
- top_bound: float32 [2], P('temp'), parts along dimension 0, may hold values from 2.2 to 3.2
Outputs:
- filtered_first: bfloat16 [32768, 128], P(('temp', 'row', 'col')), parts along dimension 0
- filtered: bfloat16 [32768, 128], P(('temp', 'row', 'col')), parts along dimension 0
The draws below stay inside these ranges and needn't reach their ends.
There are 2 independent parts, one for each index of `temp`. The reference program is written for one: setup_inputs(seed, part) draws one part's arguments, and reference() takes and returns one part's arrays. A program takes and returns all parts, laid end to end along the dimension named above; an argument that names none is the same for every part. Nothing has to cross between parts.
Inputs may be any that keep to these rules, and one draw needn't show every extreme that they name: `tile_blocks`: for grid cell d = p * 4 + q, slots 0 to 1 hold the diagonal pairs (d * 2 + k, d * 2 + k); the other live slots hold distinct pairs (i, j) with i < j, p * 8 <= i < p * 8 + 8, and j = s * 8 + q * 2 + k with 0 <= k < 2; slots from tile_count[d] on repeat the first diagonal pair. `tile_count`: every cell of the first grid row holds 24 live tiles.
All inputs are finite; a program needn't handle non-finite values.
Results may differ from the reference program's by a relative error of at most 0.013.
Values may be sent and summed in bfloat16 or wider, within the bound.
A program may use at most 128 MiB of HBM per device.

```python
import jax
import jax.numpy as jnp
from jax import lax

B = 512
NV = 128
BLK_DEV = 2
TILES_DEV = 24
NBLK = 32
NORB = 16384
N_ROW = 4
N_COL = 4


def tile_layout(key):
    devices = N_ROW * N_COL
    row_span = BLK_DEV * N_COL
    col_span = BLK_DEV * N_ROW
    places = row_span * col_span
    key = jax.random.fold_in(key, 17)
    count_key, place_key = jax.random.split(key)
    device_ids = jnp.arange(devices, dtype=jnp.int32)
    row_ids = device_ids // N_COL
    col_ids = device_ids % N_COL

    def one_device(sub_key, row_id, col_id):
        position_order = jax.random.permutation(sub_key, places).astype(jnp.int32)
        first_block = row_id * row_span + position_order // col_span
        col_local = position_order % col_span
        second_block = col_local // BLK_DEV * row_span + col_id * BLK_DEV + col_local % BLK_DEV
        is_lower = (first_block >= second_block).astype(jnp.int32)
        sorted_places = jnp.argsort(is_lower * places + jnp.arange(places, dtype=jnp.int32), stable=True)
        chosen = sorted_places[:TILES_DEV - BLK_DEV]
        return (first_block[chosen], second_block[chosen], places - jnp.sum(is_lower))
    sub_keys = jax.random.split(place_key, devices)
    first_set, second_set, valid_total = jax.vmap(one_device)(sub_keys, row_ids, col_ids)
    count_limit = BLK_DEV + 1 + (TILES_DEV - BLK_DEV) * (N_ROW - row_ids) // N_ROW
    drawn_counts = jax.random.randint(count_key, (devices,), BLK_DEV, count_limit)
    live_counts = jnp.where(row_ids == 0, TILES_DEV, jnp.minimum(drawn_counts, BLK_DEV + valid_total)).astype(jnp.int32)
    own_blocks = (device_ids * BLK_DEV)[:, None] + jnp.arange(BLK_DEV, dtype=jnp.int32)[None, :]
    rows_all = jnp.concatenate([own_blocks, first_set], axis=1)
    cols_all = jnp.concatenate([own_blocks, second_set], axis=1)
    is_live = jnp.arange(TILES_DEV, dtype=jnp.int32)[None, :] < live_counts[:, None]
    rows_all = jnp.where(is_live, rows_all, own_blocks[:, :1])
    cols_all = jnp.where(is_live, cols_all, own_blocks[:, :1])
    pairs = jnp.stack([rows_all, cols_all], axis=2).astype(jnp.int32)
    return (pairs, live_counts)


def draw_tile_blocks(key, part):
    pairs, live_counts = tile_layout(key)
    return pairs


def draw_tile_count(key, part):
    pairs, live_counts = tile_layout(key)
    return live_counts


def draw_hamiltonian(key, part):
    key = jax.random.fold_in(key, 5)
    tile_shape = (N_ROW * N_COL, TILES_DEV, B, B)
    spread_scale = (6.0 * B) ** (-0.5)
    raw_draw = jax.random.normal(key, tile_shape, jnp.float32)
    diagonal_part = raw_draw[:, :BLK_DEV]
    symmetric = (diagonal_part + jnp.swapaxes(diagonal_part, 2, 3)) * 0.70710678
    tiles = jnp.concatenate([symmetric, raw_draw[:, BLK_DEV:]], axis=1) * spread_scale
    return tiles.reshape(N_ROW * N_COL * TILES_DEV, B, B).astype(jnp.bfloat16)


def block_levels(stream_key, shape, shards, low, top_value):
    loudness = 1.0
    for dim, blocks in shards:
        heights = jax.random.uniform(jax.random.fold_in(jax.random.fold_in(stream_key, 6), dim), (blocks,), jnp.float32, low / len(shards), top_value / len(shards))
        loudness = loudness * jnp.repeat(jnp.exp(heights), shape[dim] // blocks).reshape((-1,) + (1,) * (len(shape) - 1 - dim))
    return loudness


def bell_draw(rng, dims, width, bound, shards=(), kind=jnp.bfloat16):
    values = jax.random.normal(rng, dims, jnp.float32) * width
    if len(shards) > 0:
        values = block_levels(rng, dims, shards, -0.22, 0.18) * values
    return jnp.clip(values, min=-bound, max=bound).astype(kind)


def setup_inputs(seed: int = 0, part: int = 0) -> dict:
    streams_of = jax.random.split(jax.random.key(seed), 7)
    own_keys = jax.random.split(jax.random.fold_in(streams_of[6], part), 7)
    subspace = bell_draw(own_keys[0], (NORB, NV), 1.0, 6.0, ((0, 16),))
    hamiltonian = draw_hamiltonian(jax.random.fold_in(jax.random.fold_in(streams_of[6], part), 71), part)
    tile_blocks = draw_tile_blocks(jax.random.fold_in(streams_of[6], 71), part)
    tile_count = draw_tile_count(jax.random.fold_in(streams_of[6], 71), part)
    cut_bound = jnp.clip(jax.random.uniform(own_keys[4], (1,), jnp.float32, -0.6, 0.2), -0.6, 0.2)
    top_bound = jnp.clip(jax.random.uniform(own_keys[5], (1,), jnp.float32, 2.2, 3.2), 2.2, 3.2)
    return {"subspace": subspace, "hamiltonian": hamiltonian, "tile_blocks": tile_blocks, "tile_count": tile_count, "cut_bound": cut_bound, "top_bound": top_bound}


def apply_operator(blocks, hamiltonian, tile_blocks, tile_count):
    row_span = BLK_DEV * N_COL
    tile_stack = hamiltonian.reshape(N_ROW * N_COL, TILES_DEV, B, B)
    slot_ids = jnp.arange(TILES_DEV, dtype=jnp.int32)

    def device_step(summed_all, inputs):
        tile_set, pair_set, live_total, device = inputs
        row_id = device // N_COL
        col_id = device % N_COL

        def slot_step(partials_in, slot_in):
            tile_block, tile_pair, slot_index = slot_in
            first_block = tile_pair[0]
            second_block = tile_pair[1]

            def add_tile(partials):
                row_part, col_part = partials
                local_row = first_block - row_id * row_span
                local_col = (second_block // row_span) * BLK_DEV + second_block % BLK_DEV
                right_block = lax.dynamic_index_in_dim(blocks, second_block, 0, keepdims=False)
                left_block = lax.dynamic_index_in_dim(blocks, first_block, 0, keepdims=False)
                forward = jnp.dot(tile_block, right_block, preferred_element_type=jnp.float32)
                mirror = jnp.dot(tile_block.T, left_block, preferred_element_type=jnp.float32)
                mirror = mirror * (first_block != second_block).astype(jnp.float32)
                row_part = row_part.at[local_row].add(forward)
                col_part = col_part.at[local_col].add(mirror)
                return row_part, col_part

            def keep_same(partials):
                return partials

            return lax.cond(slot_index < live_total, add_tile, keep_same, partials_in), None

        row_zero = jnp.zeros((row_span, B, NV), jnp.float32)
        col_zero = jnp.zeros((BLK_DEV * N_ROW, B, NV), jnp.float32)
        (row_part, col_part), unused = lax.scan(slot_step, (row_zero, col_zero), (tile_set, pair_set, slot_ids))
        row_round = lax.optimization_barrier(row_part.astype(jnp.bfloat16)).astype(jnp.float32)
        col_round = lax.optimization_barrier(col_part.astype(jnp.bfloat16)).astype(jnp.float32)
        summed_all = summed_all.at[row_id].add(row_round.reshape(N_COL, BLK_DEV, B, NV))
        summed_all = summed_all.at[:, col_id].add(col_round.reshape(N_ROW, BLK_DEV, B, NV))
        return summed_all, None

    zero_field = jnp.zeros((N_ROW, N_COL, BLK_DEV, B, NV), jnp.float32)
    devices = jnp.arange(N_ROW * N_COL, dtype=jnp.int32)
    summed_all, unused = lax.scan(device_step, zero_field, (tile_stack, tile_blocks, tile_count, devices))
    return summed_all.reshape(NORB, NV)


def reference(subspace, hamiltonian, tile_blocks, tile_count, cut_bound, top_bound):
    center = (cut_bound[0] + top_bound[0]) * 0.5
    half_width = (top_bound[0] - cut_bound[0]) * 0.5
    vectors32 = subspace.astype(jnp.float32)
    image_one = apply_operator(subspace.reshape(NBLK, B, NV), hamiltonian, tile_blocks, tile_count)
    filtered_first = ((image_one - center * vectors32) / half_width).astype(jnp.bfloat16)
    first_wide = lax.optimization_barrier(filtered_first).astype(jnp.float32)
    image_two = apply_operator(filtered_first.reshape(NBLK, B, NV), hamiltonian, tile_blocks, tile_count)
    filtered = ((2.0 / half_width) * (image_two - center * first_wide) - vectors32).astype(jnp.bfloat16)
    return filtered_first, filtered
```

```python
import functools

import jax
import jax.numpy as jnp
from jax import lax
from jax.experimental import pallas as pl
from jax.experimental.pallas import tpu as pltpu
from jax.sharding import PartitionSpec as P

MESH = pl.DeviceIdType.MESH
F32 = jnp.float32
BF16 = jnp.bfloat16
LANES = 128


def kernel(
    n_row, n_col, per, block, width, slots,
    tab, cut, top, v_ref, t_hbm, out1, out2,
    tbuf, prod, colset0, colset1, rowset0, rowset1, rb, rsr0, rsr1, cb, crecv0, crecv1, accr, acct,
    tsem, ag_s, ag_r, xv_s, xv_r, rs_s, rs_r, xc_s, xc_r,
):
    temp = lax.axis_index("temp")
    p = lax.axis_index("row")
    q = lax.axis_index("col")
    row_span = per * n_col
    col_span = per * n_row
    colset = (colset0, colset1)
    rowset = (rowset0, rowset1)
    rsr = (rsr0, rsr1)
    crecv = (crecv0, crecv1)
    row_table = 2 * slots
    col_table = row_table + row_span * col_span
    has_left = q > 0
    has_right = q < n_col - 1

    def tile_copy(t):
        return pltpu.make_async_copy(t_hbm.at[t], tbuf.at[t], tsem.at[t])

    def start_tile(t, carry):
        tile_copy(t).start()
        return carry

    lax.fori_loop(0, slots, start_tile, 0)

    barrier = pltpu.get_barrier_semaphore()
    for s in range(n_row):
        @pl.when(s != p)
        def _():
            pl.semaphore_signal(barrier, inc=1, device_id=(temp, s, q), device_id_type=MESH)

    @pl.when(has_left)
    def _():
        pl.semaphore_signal(barrier, inc=1, device_id=(temp, p, q - 1), device_id_type=MESH)

    @pl.when(has_right)
    def _():
        pl.semaphore_signal(barrier, inc=1, device_id=(temp, p, q + 1), device_id_type=MESH)

    pl.semaphore_wait(barrier, n_row - 1 + has_left.astype(jnp.int32) + has_right.astype(jnp.int32))

    center = (cut[0] + top[0]) * 0.5
    half_width = (top[0] - cut[0]) * 0.5

    def ag_copy(a, direction, b, to):
        return pltpu.make_async_remote_copy(
            src_ref=rowset[a].at[b], dst_ref=rowset[a].at[b],
            send_sem=ag_s.at[a, direction, b], recv_sem=ag_r.at[a, b],
            device_id=(temp, p, to), device_id_type=MESH,
        )

    def xv_copy(a, b, to, h):
        return pltpu.make_async_remote_copy(
            src_ref=colset[a].at[b], dst_ref=colset[a].at[b],
            send_sem=xv_s.at[a, to * per + h], recv_sem=xv_r.at[a, b],
            device_id=(temp, to, q), device_id_type=MESH,
        )

    def rs_copy(a, d, h, slot, to):
        return pltpu.make_async_remote_copy(
            src_ref=rb.at[d * per + h], dst_ref=rsr[a].at[slot * per + h],
            send_sem=rs_s.at[a, d * per + h], recv_sem=rs_r.at[a, slot * per + h],
            device_id=(temp, p, to), device_id_type=MESH,
        )

    def xc_copy(a, d, h, source, to):
        return pltpu.make_async_remote_copy(
            src_ref=cb.at[d * per + h], dst_ref=crecv[a].at[source * per + h],
            send_sem=xc_s.at[a, d * per + h], recv_sem=xc_r.at[a, source * per + h],
            device_id=(temp, to, q), device_id_type=MESH,
        )

    def ag_step(a, k, h):
        low = q - k
        high = q + k

        @pl.when(low >= 0)
        def _():
            b = low * per + h
            if k > 0:
                ag_copy(a, 0, b, q).wait_recv()
            if k < n_col - 1:
                @pl.when(has_right)
                def _():
                    ag_copy(a, 0, b, q + 1).start()

        @pl.when(high < n_col)
        def _():
            b = high * per + h
            if k > 0:
                ag_copy(a, 1, b, q).wait_recv()
            if k < n_col - 1:
                @pl.when(has_left)
                def _():
                    ag_copy(a, 1, b, q - 1).start()

    def send_vectors(a, h, value):
        colset[a][p * per + h] = value
        for s in range(n_row - 1):
            @pl.when(s < p)
            def _():
                xv_copy(a, p * per + h, s, h).start()
        rowset[a][q * per + h] = value.astype(F32).T.astype(BF16)
        ag_step(a, 0, h)

    def row_products(a):
        def one(t, carry):
            if a == 0:
                tile_copy(t).wait()
            prod[t] = jnp.dot(tbuf[t], colset[a][tab[t]], preferred_element_type=F32)
            return carry

        lax.fori_loop(0, slots, one, 0)

        def total(i, carry):
            base = row_table + i * col_span
            ids = [tab[base + c] for c in range(col_span)]
            for m in range(block // LANES):
                rows = pl.ds(m * LANES, LANES)
                acc = prod[ids[0], rows, :]
                for c in range(1, col_span):
                    acc = acc + prod[ids[c], rows, :]
                rb[i, rows, :] = acc.astype(BF16)
            return carry

        lax.fori_loop(0, row_span, total, 0)

    def col_products(a):
        def one(t, carry):
            out = jnp.dot(rowset[a][tab[slots + t]], tbuf[t], preferred_element_type=F32)
            for m in range(block // LANES):
                prod[t, m * width:(m + 1) * width, :] = out[:, m * LANES:(m + 1) * LANES]
            return carry

        lax.fori_loop(0, slots, one, 0)

        def total(c, carry):
            ids = [tab[col_table + r * col_span + c] for r in range(row_span)]
            for m in range(block // LANES):
                rows = pl.ds(m * width, width)
                acc = prod[ids[0], rows, :]
                for r in range(1, row_span):
                    acc = acc + prod[ids[r], rows, :]
                cb[c, :, m * LANES:(m + 1) * LANES] = acc.astype(BF16)
            return carry

        lax.fori_loop(p * per, col_span, total, 0)

    def rs_step(a, tau):
        for h in range(per):
            @pl.when(jnp.logical_and(has_right, tau >= q))
            def _():
                d = n_col - 1 - tau + q

                @pl.when(has_left)
                def _():
                    rs_copy(a, d, h, d + 1, q).wait_recv()
                    mine = rb[d * per + h].astype(F32)
                    rb[d * per + h] = (mine + rsr[a][(d + 1) * per + h].astype(F32)).astype(BF16)

                rs_copy(a, d, h, d + 1, q + 1).start()

            @pl.when(jnp.logical_and(has_left, tau >= n_col - 1 - q))
            def _():
                d = tau - (n_col - 1 - q)

                @pl.when(has_right)
                def _():
                    rs_copy(a, d, h, d, q).wait_recv()
                    mine = rb[d * per + h].astype(F32)
                    rb[d * per + h] = (mine + rsr[a][d * per + h].astype(F32)).astype(BF16)

                rs_copy(a, d, h, d, q - 1).start()

    def wait_rs_sends(a):
        for d in range(n_col):
            @pl.when(d != q)
            def _():
                for h in range(per):
                    rs_copy(a, d, h, d, q).wait_send()

    def wait_xc_sends(a):
        for s in range(1, n_row):
            @pl.when(s > p)
            def _():
                for h in range(per):
                    xc_copy(a, s, h, p, s).wait_send()

    def wait_vector_sends(a):
        for s in range(n_row - 1):
            @pl.when(s < p)
            def _():
                for h in range(per):
                    xv_copy(a, p * per + h, s, h).wait_send()
        for b in range(n_col):
            for h in range(per):
                @pl.when(jnp.logical_and(has_right, b <= q))
                def _():
                    ag_copy(a, 0, b * per + h, q).wait_send()

                @pl.when(jnp.logical_and(has_left, b >= q))
                def _():
                    ag_copy(a, 1, b * per + h, q).wait_send()

    def image(a, h):
        acct[...] = cb[p * per + h].astype(F32)
        for s in range(n_row - 1):
            @pl.when(s < p)
            def _():
                xc_copy(a, p, h, s, p).wait_recv()
                acct[...] += crecv[a][s * per + h].astype(F32)
        accr[...] = rb[q * per + h].astype(F32) + acct[...].T

        @pl.when(has_left)
        def _():
            rs_copy(a, q, h, q + 1, q).wait_recv()
            accr[...] += rsr[a][(q + 1) * per + h].astype(F32)

        @pl.when(has_right)
        def _():
            rs_copy(a, q, h, q, q).wait_recv()
            accr[...] += rsr[a][q * per + h].astype(F32)

        return accr[...]

    def apply(a):
        for k in range(1, n_col - 1):
            for h in range(per):
                ag_step(a, k, h)
        for s in range(1, n_row):
            @pl.when(s > p)
            def _():
                for h in range(per):
                    xv_copy(a, s * per + h, 0, h).wait_recv()
        if a > 0:
            wait_rs_sends(a - 1)
        row_products(a)
        rs_step(a, 0)
        for h in range(per):
            ag_step(a, n_col - 1, h)
        if a > 0:
            wait_xc_sends(a - 1)
        col_products(a)
        for s in range(n_row - 1, 0, -1):
            @pl.when(s > p)
            def _():
                for h in range(per):
                    xc_copy(a, s, h, p, s).start()

        def step(tau, carry):
            rs_step(a, tau)
            return carry

        lax.fori_loop(1, n_col - 1, step, 0)

    prod[slots] = jnp.zeros((block, width), F32)
    for h in range(per):
        send_vectors(0, h, v_ref[h * block:(h + 1) * block, :])
    apply(0)
    for h in range(per):
        rows = pl.ds(h * block, block)
        vectors = v_ref[rows, :].astype(F32)
        first = ((image(0, h) - center * vectors) / half_width).astype(BF16)
        out1[rows, :] = first
        send_vectors(1, h, first)
    apply(1)
    for h in range(per):
        rows = pl.ds(h * block, block)
        vectors = v_ref[rows, :].astype(F32)
        first = out1[rows, :].astype(F32)
        out2[rows, :] = (2.0 * (image(1, h) - center * first) / half_width - vectors).astype(BF16)
    wait_rs_sends(1)
    wait_xc_sends(1)
    wait_vector_sends(0)
    wait_vector_sends(1)


def body(subspace, hamiltonian, tile_blocks, tile_count, cut_bound, top_bound):
    block = hamiltonian.shape[1]
    width = subspace.shape[1]
    slots = hamiltonian.shape[0]
    per = subspace.shape[0] // block
    n_row = lax.axis_size("row")
    n_col = lax.axis_size("col")
    row_span = per * n_col
    col_span = per * n_row
    first = tile_blocks[0, :, 0]
    second = tile_blocks[0, :, 1]
    local_rows = first - lax.axis_index("row") * row_span
    local_cols = second // row_span * per + second % per
    slot_ids = jnp.arange(slots, dtype=jnp.int32)
    live = slot_ids < tile_count[0]
    place = local_rows * col_span + local_cols
    places = jnp.arange(row_span * col_span, dtype=jnp.int32)
    hit = jnp.logical_and(places[:, None] == place[None, :], live[None, :])
    row_slot = jnp.min(jnp.where(hit, slot_ids[None, :], slots), axis=1)
    upper = jnp.logical_and(hit, (first != second)[None, :])
    col_slot = jnp.min(jnp.where(upper, slot_ids[None, :], slots), axis=1)
    tab = jnp.concatenate([local_cols, local_rows, row_slot, col_slot])

    vmem = functools.partial(pl.BlockSpec, memory_space=pltpu.VMEM)
    smem = functools.partial(pl.BlockSpec, memory_space=pltpu.SMEM)
    cols = pltpu.VMEM((col_span, block, width), BF16)
    rows = pltpu.VMEM((row_span, width, block), BF16)
    arrivals = pltpu.VMEM((row_span + per, block, width), BF16)
    col_terms = pltpu.VMEM((col_span, width, block), BF16)
    dma = pltpu.SemaphoreType.DMA
    shape = jax.ShapeDtypeStruct(subspace.shape, BF16)
    return pl.pallas_call(
        functools.partial(kernel, n_row, n_col, per, block, width, slots),
        out_shape=(shape, shape),
        in_specs=[smem(), smem(), smem(), vmem(), pl.BlockSpec(memory_space=pl.ANY)],
        out_specs=(vmem(), vmem()),
        scratch_shapes=[
            pltpu.VMEM((slots, block, block), BF16),
            pltpu.VMEM((slots + 1, block, width), F32),
            cols, cols, rows, rows,
            pltpu.VMEM((row_span, block, width), BF16),
            arrivals, arrivals,
            col_terms, col_terms, col_terms,
            pltpu.VMEM((block, width), F32),
            pltpu.VMEM((width, block), F32),
            dma((slots,)),
            dma((2, 2, row_span)),
            dma((2, row_span)),
            dma((2, col_span)),
            dma((2, col_span)),
            dma((2, row_span)),
            dma((2, row_span + per)),
            dma((2, col_span)),
            dma((2, col_span)),
        ],
        compiler_params=pltpu.CompilerParams(
            collective_id=0, has_side_effects=True, vmem_limit_bytes=60 * 1024 * 1024
        ),
    )(tab, cut_bound, top_bound, subspace, hamiltonian)


def solution(mesh):
    return jax.shard_map(
        body,
        mesh=mesh,
        in_specs=(
            P(("temp", "row", "col"), None),
            P(("temp", "row", "col"), None, None),
            P(("row", "col"), None, None),
            P(("row", "col")),
            P("temp"),
            P("temp"),
        ),
        out_specs=(P(("temp", "row", "col"), None), P(("temp", "row", "col"), None)),
        check_vma=False,
    )
```

```python
import functools

import jax
import jax.numpy as jnp
from jax import lax
from jax.experimental import pallas as pl
from jax.experimental.pallas import tpu as pltpu
from jax.sharding import PartitionSpec as P

MESH = pl.DeviceIdType.MESH
F32 = jnp.float32
BF16 = jnp.bfloat16
LANES = 128
UNROLL = 4


def kernel(
    n_row, n_col, per, block, width, slots,
    pairs, count, cut, top, v_ref, t_hbm, out1, out2,
    tbuf, prod, colset0, colset1, rowset0, rowset1, rb, rsr0, rsr1, cb, crecv0, crecv1, accr, acct,
    keys, vec_slot, row_slot, col_slot, tsem, ag_s, ag_r, xv_s, xv_r, rs_s, rs_r, xc_s, xc_r,
):
    temp = lax.axis_index("temp")
    p = lax.axis_index("row")
    q = lax.axis_index("col")
    row_span = per * n_col
    col_span = per * n_row
    colset = (colset0, colset1)
    rowset = (rowset0, rowset1)
    rsr = (rsr0, rsr1)
    crecv = (crecv0, crecv1)
    core = lax.rem(p, 2)
    chip = p // 2
    sib = p + 1 - 2 * core
    chips = n_row // 2
    has_left = q > 0
    has_right = q < n_col - 1

    def tile_copy(t):
        return pltpu.make_async_copy(t_hbm.at[t], tbuf.at[t], tsem.at[t])

    def start_tile(t, carry):
        tile_copy(t).start()
        return carry

    lax.fori_loop(0, slots, start_tile, 0)

    barrier = pltpu.get_barrier_semaphore()
    for s in range(n_row):
        @pl.when(s != p)
        def _():
            pl.semaphore_signal(barrier, inc=1, device_id=(temp, s, q), device_id_type=MESH)

    @pl.when(has_left)
    def _():
        pl.semaphore_signal(barrier, inc=1, device_id=(temp, p, q - 1), device_id_type=MESH)

    @pl.when(has_right)
    def _():
        pl.semaphore_signal(barrier, inc=1, device_id=(temp, p, q + 1), device_id_type=MESH)

    pl.semaphore_wait(barrier, n_row - 1 + has_left.astype(jnp.int32) + has_right.astype(jnp.int32))

    center = (cut[0] + top[0]) * 0.5
    half_width = (top[0] - cut[0]) * 0.5

    def ag_copy(a, direction, b, to):
        return pltpu.make_async_remote_copy(
            src_ref=rowset[a].at[b], dst_ref=rowset[a].at[b],
            send_sem=ag_s.at[a, direction, b], recv_sem=ag_r.at[a, b],
            device_id=(temp, p, to), device_id_type=MESH,
        )

    def xv_copy(a, b, to, h):
        return pltpu.make_async_remote_copy(
            src_ref=colset[a].at[b], dst_ref=colset[a].at[b],
            send_sem=xv_s.at[a, to * per + h], recv_sem=xv_r.at[a, b],
            device_id=(temp, to, q), device_id_type=MESH,
        )

    def rs_copy(a, d, h, slot, to):
        return pltpu.make_async_remote_copy(
            src_ref=rb.at[d * per + h], dst_ref=rsr[a].at[slot * per + h],
            send_sem=rs_s.at[a, d * per + h], recv_sem=rs_r.at[a, slot * per + h],
            device_id=(temp, p, to), device_id_type=MESH,
        )

    def xc_copy(a, d, h, source, to):
        return pltpu.make_async_remote_copy(
            src_ref=cb.at[d * per + h], dst_ref=crecv[a].at[source * per + h],
            send_sem=xc_s.at[a, d * per + h], recv_sem=xc_r.at[a, source * per + h],
            device_id=(temp, to, q), device_id_type=MESH,
        )

    def ag_step(a, k, h):
        low = q - k
        high = q + k

        @pl.when(low >= 0)
        def _():
            b = low * per + h
            if k > 0:
                ag_copy(a, 0, b, q).wait_recv()
            if k < n_col - 1:
                @pl.when(has_right)
                def _():
                    ag_copy(a, 0, b, q + 1).start()

        @pl.when(high < n_col)
        def _():
            b = high * per + h
            if k > 0:
                ag_copy(a, 1, b, q).wait_recv()
            if k < n_col - 1:
                @pl.when(has_left)
                def _():
                    ag_copy(a, 1, b, q - 1).start()

    def later_chips(fn):
        for x in range(1, chips):
            @pl.when(x > chip)
            def _():
                fn(x)

    def earlier_chips(fn):
        for x in range(chips - 1):
            @pl.when(x < chip)
            def _():
                fn(x)

    def send_vectors(a, h, value):
        mine = p * per + h
        colset[a][mine] = value
        earlier_chips(lambda x: xv_copy(a, mine, 2 * x + core, h).start())

        @pl.when(core == 1)
        def _():
            xv_copy(a, mine, sib, h).start()

        rowset[a][q * per + h] = value.astype(F32).T.astype(BF16)
        ag_step(a, 0, h)

    def forward_copy(a, x, h):
        s = 2 * x + core
        return pltpu.make_async_remote_copy(
            src_ref=colset[a].at[s * per + h], dst_ref=colset[a].at[s * per + h],
            send_sem=xv_s.at[a, s * per + h], recv_sem=xv_r.at[a, s * per + h],
            device_id=(temp, sib, q), device_id_type=MESH,
        )

    def finish_row_gather(a):
        for h in range(per):
            def relay(x):
                xv_copy(a, (2 * x + core) * per + h, sib, h).wait_recv()
                forward_copy(a, x, h).start()

            later_chips(relay)
        for h in range(per):
            @pl.when(core == 0)
            def _():
                xv_copy(a, sib * per + h, sib, h).wait_recv()

            later_chips(lambda x: xv_copy(a, (2 * x + 1 - core) * per + h, sib, h).wait_recv())

    def find_slots():
        for t in range(slots):
            first = pairs[0, t, 0]
            second = pairs[0, t, 1]
            local_row = first - p * row_span
            local_col = second // row_span * per + lax.rem(second, per)
            vec_slot[t] = jnp.clip(local_col, 0, col_span - 1)
            vec_slot[slots + t] = jnp.clip(local_row, 0, row_span - 1)
            keys[t] = jnp.where(t < count[0], local_row * col_span + local_col, -1)
        held = [keys[t] for t in range(slots)]

        def find(i, carry):
            slot = jnp.int32(slots)
            for t in range(slots):
                slot = jnp.where(held[t] == i, t, slot)
            row_slot[i] = slot
            col_slot[i] = slot
            return carry

        lax.fori_loop(0, row_span * col_span, find, 0)
        for k in range(per):
            col_slot[(q * per + k) * col_span + p * per + k] = slots

    def grouped(lo, hi, one):
        group = UNROLL if (hi - lo) % UNROLL == 0 else 1

        def several(g, carry):
            for u in range(group):
                one(lo + g * group + u)
            return carry

        lax.fori_loop(0, (hi - lo) // group, several, 0)

    def row_products(a, lo, hi):
        def one(t):
            if a == 0:
                tile_copy(t).wait()
            prod[t] = jnp.dot(tbuf[t], colset[a][vec_slot[t]], preferred_element_type=F32)

        grouped(lo, hi, one)

    def row_totals():
        def total(i, carry):
            ids = [row_slot[i * col_span + c] for c in range(col_span)]
            for m in range(block // LANES):
                rows = pl.ds(m * LANES, LANES)
                acc = prod[ids[0], rows, :]
                for c in range(1, col_span):
                    acc = acc + prod[ids[c], rows, :]
                rb[i, rows, :] = acc.astype(BF16)
            return carry

        lax.fori_loop(0, row_span, total, 0)

    def col_products(a):
        def one(t):
            out = jnp.dot(rowset[a][vec_slot[slots + t]], tbuf[t], preferred_element_type=F32)
            for m in range(block // LANES):
                prod[t, m * width:(m + 1) * width, :] = out[:, m * LANES:(m + 1) * LANES]

        grouped(0, slots, one)

    def col_totals():
        def total(c, carry):
            ids = [col_slot[r * col_span + c] for r in range(row_span)]
            for m in range(block // LANES):
                rows = pl.ds(m * width, width)
                acc = prod[ids[0], rows, :]
                for r in range(1, row_span):
                    acc = acc + prod[ids[r], rows, :]
                cb[c, :, m * LANES:(m + 1) * LANES] = acc.astype(BF16)
            return carry

        lax.fori_loop(p * per, col_span, total, 0)

    def send_col_sums(a):
        @pl.when(core == 0)
        def _():
            for h in range(per):
                xc_copy(a, sib, h, chip, sib).start()

        def to_sibling(x):
            d = 2 * x + 1 - core
            for h in range(per):
                xc_copy(a, d, h, d, sib).start()

        later_chips(to_sibling)

        def across(x):
            d = 2 * x + core
            for h in range(per):
                xc_copy(a, d, h, d, sib).wait_recv()
                mine = cb[d * per + h].astype(F32)
                cb[d * per + h] = (mine + crecv[a][d * per + h].astype(F32)).astype(BF16)
                xc_copy(a, d, h, chip, d).start()

        later_chips(across)

    def rs_step(a, tau):
        for h in range(per):
            @pl.when(jnp.logical_and(has_right, tau >= q))
            def _():
                d = n_col - 1 - tau + q

                @pl.when(has_left)
                def _():
                    rs_copy(a, d, h, d + 1, q).wait_recv()
                    mine = rb[d * per + h].astype(F32)
                    rb[d * per + h] = (mine + rsr[a][(d + 1) * per + h].astype(F32)).astype(BF16)

                rs_copy(a, d, h, d + 1, q + 1).start()

            @pl.when(jnp.logical_and(has_left, tau >= n_col - 1 - q))
            def _():
                d = tau - (n_col - 1 - q)

                @pl.when(has_right)
                def _():
                    rs_copy(a, d, h, d, q).wait_recv()
                    mine = rb[d * per + h].astype(F32)
                    rb[d * per + h] = (mine + rsr[a][d * per + h].astype(F32)).astype(BF16)

                rs_copy(a, d, h, d, q - 1).start()

    def wait_rs_sends(a):
        for d in range(n_col):
            @pl.when(d != q)
            def _():
                for h in range(per):
                    rs_copy(a, d, h, d, q).wait_send()

    def wait_xc_sends(a):
        for s in range(1, n_row):
            @pl.when(s > p)
            def _():
                for h in range(per):
                    xc_copy(a, s, h, p, s).wait_send()

    def wait_vector_sends(a):
        for h in range(per):
            earlier_chips(lambda x: xv_copy(a, p * per + h, 2 * x + core, h).wait_send())

            @pl.when(core == 1)
            def _():
                xv_copy(a, p * per + h, sib, h).wait_send()

            later_chips(lambda x: forward_copy(a, x, h).wait_send())
        for b in range(n_col):
            for h in range(per):
                @pl.when(jnp.logical_and(has_right, b <= q))
                def _():
                    ag_copy(a, 0, b * per + h, q).wait_send()

                @pl.when(jnp.logical_and(has_left, b >= q))
                def _():
                    ag_copy(a, 1, b * per + h, q).wait_send()

    def image(a, h):
        acct[...] = cb[p * per + h].astype(F32)

        def add(x):
            xc_copy(a, p, h, x, p).wait_recv()
            acct[...] += crecv[a][x * per + h].astype(F32)

        @pl.when(core == 1)
        def _():
            add(chip)

        earlier_chips(add)
        accr[...] = rb[q * per + h].astype(F32) + acct[...].T

        @pl.when(has_left)
        def _():
            rs_copy(a, q, h, q + 1, q).wait_recv()
            accr[...] += rsr[a][(q + 1) * per + h].astype(F32)

        @pl.when(has_right)
        def _():
            rs_copy(a, q, h, q, q).wait_recv()
            accr[...] += rsr[a][q * per + h].astype(F32)

        return accr[...]

    def apply(a):
        for h in range(per):
            ag_step(a, 1, h)
        finish_row_gather(a)
        row_products(a, 0, slots // 2)
        for k in range(2, n_col - 1):
            for h in range(per):
                ag_step(a, k, h)
        row_products(a, slots // 2, slots)
        if a > 0:
            wait_rs_sends(a - 1)
        row_totals()
        rs_step(a, 0)
        for h in range(per):
            ag_step(a, n_col - 1, h)
        if a > 0:
            wait_xc_sends(a - 1)
        rs_step(a, 1)
        col_products(a)
        col_totals()
        send_col_sums(a)

        def step(tau, carry):
            rs_step(a, tau)
            return carry

        lax.fori_loop(2, n_col - 1, step, 0)

    prod[slots] = jnp.zeros((block, width), F32)
    for h in range(per):
        send_vectors(0, h, v_ref[h * block:(h + 1) * block, :])
    find_slots()
    apply(0)
    for h in range(per):
        rows = pl.ds(h * block, block)
        vectors = v_ref[rows, :].astype(F32)
        first = ((image(0, h) - center * vectors) / half_width).astype(BF16)
        out1[rows, :] = first
        send_vectors(1, h, first)
    apply(1)
    for h in range(per):
        rows = pl.ds(h * block, block)
        vectors = v_ref[rows, :].astype(F32)
        first = out1[rows, :].astype(F32)
        out2[rows, :] = (2.0 * (image(1, h) - center * first) / half_width - vectors).astype(BF16)
    wait_rs_sends(1)
    wait_xc_sends(1)
    wait_vector_sends(0)
    wait_vector_sends(1)


def body(subspace, hamiltonian, tile_blocks, tile_count, cut_bound, top_bound):
    block = hamiltonian.shape[1]
    width = subspace.shape[1]
    slots = hamiltonian.shape[0]
    per = subspace.shape[0] // block
    n_row = lax.axis_size("row")
    n_col = lax.axis_size("col")
    row_span = per * n_col
    col_span = per * n_row
    vmem = functools.partial(pl.BlockSpec, memory_space=pltpu.VMEM)
    smem = functools.partial(pl.BlockSpec, memory_space=pltpu.SMEM)
    cols = pltpu.VMEM((col_span, block, width), BF16)
    rows = pltpu.VMEM((row_span, width, block), BF16)
    arrivals = pltpu.VMEM((row_span + per, block, width), BF16)
    col_terms = pltpu.VMEM((col_span, width, block), BF16)
    dma = pltpu.SemaphoreType.DMA
    shape = jax.ShapeDtypeStruct(subspace.shape, BF16)
    return pl.pallas_call(
        functools.partial(kernel, n_row, n_col, per, block, width, slots),
        out_shape=(shape, shape),
        in_specs=[smem(), smem(), smem(), smem(), vmem(), pl.BlockSpec(memory_space=pl.ANY)],
        out_specs=(vmem(), vmem()),
        scratch_shapes=[
            pltpu.VMEM((slots, block, block), BF16),
            pltpu.VMEM((slots + 1, block, width), F32),
            cols, cols, rows, rows,
            pltpu.VMEM((row_span, block, width), BF16),
            arrivals, arrivals,
            col_terms, col_terms, col_terms,
            pltpu.VMEM((block, width), F32),
            pltpu.VMEM((width, block), F32),
            pltpu.SMEM((slots,), jnp.int32),
            pltpu.SMEM((2 * slots,), jnp.int32),
            pltpu.SMEM((row_span * col_span,), jnp.int32),
            pltpu.SMEM((row_span * col_span,), jnp.int32),
            dma((slots,)),
            dma((2, 2, row_span)),
            dma((2, row_span)),
            dma((2, col_span)),
            dma((2, col_span)),
            dma((2, row_span)),
            dma((2, row_span + per)),
            dma((2, col_span)),
            dma((2, col_span)),
        ],
        compiler_params=pltpu.CompilerParams(
            collective_id=0, has_side_effects=True, vmem_limit_bytes=60 * 1024 * 1024
        ),
    )(tile_blocks, tile_count, cut_bound, top_bound, subspace, hamiltonian)


def solution(mesh):
    return jax.shard_map(
        body,
        mesh=mesh,
        in_specs=(
            P(("temp", "row", "col"), None),
            P(("temp", "row", "col"), None, None),
            P(("row", "col"), None, None),
            P(("row", "col")),
            P("temp"),
            P("temp"),
        ),
        out_specs=(P(("temp", "row", "col"), None), P(("temp", "row", "col"), None)),
        check_vma=False,
    )
```

```python
import functools

import jax
import jax.numpy as jnp
from jax import lax
from jax.experimental import pallas as pl
from jax.experimental.pallas import tpu as pltpu
from jax.sharding import PartitionSpec as P

MESH = pl.DeviceIdType.MESH
F32 = jnp.float32
BF16 = jnp.bfloat16
PIECE = 32
UNROLL = 8
HALVES = 2


def kernel(
    n_row, n_col, per, block, width, slots, turned,
    pairs, count, cut, top, v_ref, t_hbm, out1, out2,
    tbuf, tbuf_t, prod, col00, col01, col10, col11, row00, row01, row10, row11, rb, rsr0, rsr1, cb, crecv0, crecv1, acc, held32, wide,
    keys, vec_slot, row_slot, col_slot, tsem, ag_s, ag_r, xv_s, xv_r, rs_s, rs_r, xc_s, xc_r,
):
    temp = lax.axis_index("temp")
    p = lax.axis_index("row")
    q = lax.axis_index("col")
    row_span = per * n_col
    col_span = per * n_row
    colset = ((col00, col01), (col10, col11))
    rowset = ((row00, row01), (row10, row11))
    half = width // HALVES
    parts = range(HALVES)

    def span(owner):
        return pl.ds(owner * per, per)

    def lines(h):
        return pl.ds(h * half, half)

    rsr = (rsr0, rsr1)
    crecv = (crecv0, crecv1)
    core = lax.rem(p, 2)
    chip = p // 2
    sib = p + 1 - 2 * core
    chips = n_row // 2
    has_left = q > 0
    has_right = q < n_col - 1

    def tile_copy(t):
        return pltpu.make_async_copy(t_hbm.at[t], tbuf.at[t], tsem.at[t])

    def start_tile(t, carry):
        tile_copy(t).start()
        return carry

    lax.fori_loop(0, slots, start_tile, 0)

    barrier = pltpu.get_barrier_semaphore()
    for s in range(n_row):
        @pl.when(s != p)
        def _():
            pl.semaphore_signal(barrier, inc=1, device_id=(temp, s, q), device_id_type=MESH)

    @pl.when(has_left)
    def _():
        pl.semaphore_signal(barrier, inc=1, device_id=(temp, p, q - 1), device_id_type=MESH)

    @pl.when(has_right)
    def _():
        pl.semaphore_signal(barrier, inc=1, device_id=(temp, p, q + 1), device_id_type=MESH)

    pl.semaphore_wait(barrier, n_row - 1 + has_left.astype(jnp.int32) + has_right.astype(jnp.int32))

    center = (cut[0] + top[0]) * 0.5
    half_width = (top[0] - cut[0]) * 0.5

    def ag_copy(a, direction, owner, h, to):
        ref = rowset[a][h].at[span(owner)]
        return pltpu.make_async_remote_copy(
            src_ref=ref, dst_ref=ref,
            send_sem=ag_s.at[a, direction, owner * HALVES + h],
            recv_sem=ag_r.at[a, owner * HALVES + h],
            device_id=(temp, p, to), device_id_type=MESH,
        )

    def xv_copy(a, owner, to, h, send):
        ref = colset[a][h].at[span(owner)]
        return pltpu.make_async_remote_copy(
            src_ref=ref, dst_ref=ref,
            send_sem=xv_s.at[a, send * HALVES + h], recv_sem=xv_r.at[a, owner * HALVES + h],
            device_id=(temp, to, q), device_id_type=MESH,
        )

    def rs_copy(a, d, h, slot, to):
        return pltpu.make_async_remote_copy(
            src_ref=rb.at[span(d), lines(h)], dst_ref=rsr[a].at[span(slot), lines(h)],
            send_sem=rs_s.at[a, d * HALVES + h], recv_sem=rs_r.at[a, slot * HALVES + h],
            device_id=(temp, p, to), device_id_type=MESH,
        )

    def xc_copy(a, d, h, source, to):
        return pltpu.make_async_remote_copy(
            src_ref=cb.at[span(d), lines(h)], dst_ref=crecv[a].at[span(source), lines(h)],
            send_sem=xc_s.at[a, d * HALVES + h], recv_sem=xc_r.at[a, source * HALVES + h],
            device_id=(temp, to, q), device_id_type=MESH,
        )

    def ag_step(a, k, h):
        low = q - k
        high = q + k

        @pl.when(low >= 0)
        def _():
            if k > 0:
                ag_copy(a, 0, low, h, q).wait_recv()
            if k < n_col - 1:
                @pl.when(has_right)
                def _():
                    ag_copy(a, 0, low, h, q + 1).start()

        @pl.when(high < n_col)
        def _():
            if k > 0:
                ag_copy(a, 1, high, h, q).wait_recv()
            if k < n_col - 1:
                @pl.when(has_left)
                def _():
                    ag_copy(a, 1, high, h, q - 1).start()

    def later_chips(fn):
        for x in range(1, chips):
            @pl.when(x > chip)
            def _():
                fn(x)

    def earlier_chips(fn):
        for x in range(chips - 1):
            @pl.when(x < chip)
            def _():
                fn(x)

    def send_vectors(a, h, value):
        colset[a][h][span(p)] = value
        earlier_chips(lambda x: xv_copy(a, p, 2 * x + core, h, 2 * x + core).start())

        @pl.when(core == 1)
        def _():
            xv_copy(a, p, sib, h, sib).start()

        rowset[a][h][span(q)] = value
        ag_step(a, 0, h)

    def forward_copy(a, x, h):
        return xv_copy(a, 2 * x + core, sib, h, 2 * x + core)

    def finish_row_gather(a, h):
        def relay(x):
            forward_copy(a, x, h).wait_recv()
            forward_copy(a, x, h).start()

        later_chips(relay)

        @pl.when(core == 0)
        def _():
            xv_copy(a, sib, sib, h, sib).wait_recv()

        later_chips(lambda x: xv_copy(a, 2 * x + 1 - core, sib, h, sib).wait_recv())

    def find_slots():
        for t in range(slots):
            first = pairs[0, t, 0]
            second = pairs[0, t, 1]
            local_row = first - p * row_span
            local_col = second // row_span * per + lax.rem(second, per)
            vec_slot[t] = jnp.clip(local_col, 0, col_span - 1)
            vec_slot[slots + t] = jnp.clip(local_row, 0, row_span - 1)
            keys[t] = jnp.where(t < count[0], local_row * col_span + local_col, -1)
        held = [keys[t] for t in range(slots)]

        def find(i, carry):
            slot = jnp.int32(slots)
            for t in range(slots):
                slot = jnp.where(held[t] == i, t, slot)
            row_slot[i] = slot
            col_slot[i] = slot
            return carry

        lax.fori_loop(0, row_span * col_span, find, 0)
        for k in range(per):
            col_slot[(q * per + k) * col_span + p * per + k] = slots

    def grouped(lo, hi, one):
        group = UNROLL if (hi - lo) % UNROLL == 0 else 1

        def several(g, carry):
            for u in range(group):
                one(lo + g * group + u)
            return carry

        lax.fori_loop(0, (hi - lo) // group, several, 0)

    def transpose_tiles():
        def one(t, carry):
            tile_copy(t).wait()
            if turned:
                tbuf_t[t] = tbuf[t].T
            return carry

        lax.fori_loop(0, slots, one, 0)

    def row_products(a, h):
        def one(t):
            vectors = colset[a][h][vec_slot[t]]
            if turned:
                prod[t, lines(h), :] = jnp.dot(vectors, tbuf_t[t], preferred_element_type=F32)
            else:
                prod[t, lines(h), :] = lax.dot_general(
                    vectors, tbuf[t], (((1,), (1,)), ((), ())), preferred_element_type=F32
                )

        grouped(0, slots, one)

    def row_totals(h):
        def total(i, carry):
            ids = [row_slot[i * col_span + c] for c in range(col_span)]
            for m in range(half // PIECE):
                rows = pl.ds(h * half + m * PIECE, PIECE)
                acc = prod[ids[0], rows, :]
                for c in range(1, col_span):
                    acc = acc + prod[ids[c], rows, :]
                rb[i, rows, :] = acc.astype(BF16)
            return carry

        lax.fori_loop(0, row_span, total, 0)

    def col_products(a, h):
        def one(t):
            prod[t, lines(h), :] = jnp.dot(
                rowset[a][h][vec_slot[slots + t]], tbuf[t], preferred_element_type=F32
            )

        grouped(0, slots, one)

    def col_totals(h):
        def total(c, carry):
            ids = [col_slot[r * col_span + c] for r in range(row_span)]
            for m in range(half // PIECE):
                rows = pl.ds(h * half + m * PIECE, PIECE)
                acc = prod[ids[0], rows, :]
                for r in range(1, row_span):
                    acc = acc + prod[ids[r], rows, :]
                cb[c, rows, :] = acc.astype(BF16)
            return carry

        lax.fori_loop(p * per, col_span, total, 0)

    def send_to_sibling(a, h):
        @pl.when(core == 0)
        def _():
            xc_copy(a, sib, h, chip, sib).start()

        def to_sibling(x):
            d = 2 * x + 1 - core
            xc_copy(a, d, h, d, sib).start()

        later_chips(to_sibling)

    def send_across(a, h):
        def across(x):
            d = 2 * x + core
            xc_copy(a, d, h, d, sib).wait_recv()
            mine = cb[span(d), lines(h), :].astype(F32)
            cb[span(d), lines(h), :] = (mine + crecv[a][span(d), lines(h), :].astype(F32)).astype(BF16)
            xc_copy(a, d, h, chip, d).start()

        later_chips(across)

    def add_arrival(a, d, h, slot):
        rs_copy(a, d, h, slot, q).wait_recv()
        mine = rb[span(d), lines(h), :].astype(F32)
        rb[span(d), lines(h), :] = (mine + rsr[a][span(slot), lines(h), :].astype(F32)).astype(BF16)

    def rs_step(a, tau, h):
        @pl.when(jnp.logical_and(has_right, tau >= q))
        def _():
            d = n_col - 1 - tau + q

            @pl.when(has_left)
            def _():
                add_arrival(a, d, h, d + 1)

            rs_copy(a, d, h, d + 1, q + 1).start()

        @pl.when(jnp.logical_and(has_left, tau >= n_col - 1 - q))
        def _():
            d = tau - (n_col - 1 - q)

            @pl.when(has_right)
            def _():
                add_arrival(a, d, h, d)

            rs_copy(a, d, h, d, q - 1).start()

    def wait_rs_sends(a):
        for d in range(n_col):
            @pl.when(d != q)
            def _():
                for h in parts:
                    rs_copy(a, d, h, d, q).wait_send()

    def wait_xc_sends(a):
        for s in range(1, n_row):
            @pl.when(s > p)
            def _():
                for h in parts:
                    xc_copy(a, s, h, p, s).wait_send()

    def wait_vector_sends(a):
        for h in parts:
            earlier_chips(lambda x: xv_copy(a, p, 2 * x + core, h, 2 * x + core).wait_send())

            @pl.when(core == 1)
            def _():
                xv_copy(a, p, sib, h, sib).wait_send()

            later_chips(lambda x: forward_copy(a, x, h).wait_send())
            for b in range(n_col):
                @pl.when(jnp.logical_and(has_right, b <= q))
                def _():
                    ag_copy(a, 0, b, h, q).wait_send()

                @pl.when(jnp.logical_and(has_left, b >= q))
                def _():
                    ag_copy(a, 1, b, h, q).wait_send()

    def image(a, h):
        acc[...] = cb[span(p), lines(h), :].astype(F32) + rb[span(q), lines(h), :].astype(F32)

        def add(x):
            xc_copy(a, p, h, x, p).wait_recv()
            acc[...] += crecv[a][span(x), lines(h), :].astype(F32)

        @pl.when(core == 1)
        def _():
            add(chip)

        earlier_chips(add)

        @pl.when(has_left)
        def _():
            rs_copy(a, q, h, q + 1, q).wait_recv()
            acc[...] += rsr[a][span(q + 1), lines(h), :].astype(F32)

        @pl.when(has_right)
        def _():
            rs_copy(a, q, h, q, q).wait_recv()
            acc[...] += rsr[a][span(q), lines(h), :].astype(F32)

        return acc[...]

    def apply(a):
        if a == 0:
            transpose_tiles()
        else:
            wait_rs_sends(a - 1)
        for h in parts:
            ag_step(a, 1, h)
            finish_row_gather(a, h)
            row_products(a, h)
            row_totals(h)
            rs_step(a, 0, h)
        for h in parts:
            for k in range(2, n_col - 1):
                ag_step(a, k, h)
            rs_step(a, 1, h)
        if a > 0:
            wait_xc_sends(a - 1)
        for h in parts:
            ag_step(a, n_col - 1, h)
            col_products(a, h)
            col_totals(h)
            send_to_sibling(a, h)
        for h in parts:
            rs_step(a, 2, h)
            send_across(a, h)

        def step(tau, carry):
            for h in parts:
                rs_step(a, tau, h)
            return carry

        lax.fori_loop(3, n_col - 1, step, 0)

    prod[slots] = jnp.zeros((width, block), F32)
    for k in range(per):
        held32[k] = v_ref[k * block:(k + 1) * block, :].astype(F32).T
    for h in parts:
        send_vectors(0, h, held32[:, lines(h), :].astype(BF16))
    find_slots()
    apply(0)
    for h in parts:
        vectors = held32[:, lines(h), :]
        send_vectors(1, h, ((image(0, h) - center * vectors) / half_width).astype(BF16))
    for k in range(per):
        for h in parts:
            wide[lines(h), :] = colset[1][h][p * per + k].astype(F32)
        out1[k * block:(k + 1) * block, :] = wide[...].T.astype(BF16)
    apply(1)
    for h in parts:
        first = colset[1][h][span(p)].astype(F32)
        vectors = held32[:, lines(h), :]
        held32[:, lines(h), :] = 2.0 * (image(1, h) - center * first) / half_width - vectors
    for k in range(per):
        out2[k * block:(k + 1) * block, :] = held32[k].T.astype(BF16)
    wait_rs_sends(1)
    wait_xc_sends(1)
    wait_vector_sends(0)
    wait_vector_sends(1)


def body(subspace, hamiltonian, tile_blocks, tile_count, cut_bound, top_bound):
    block = hamiltonian.shape[1]
    width = subspace.shape[1]
    slots = hamiltonian.shape[0]
    per = subspace.shape[0] // block
    n_row = lax.axis_size("row")
    n_col = lax.axis_size("col")
    row_span = per * n_col
    col_span = per * n_row
    turned = row_span + col_span <= slots
    vmem = functools.partial(pl.BlockSpec, memory_space=pltpu.VMEM)
    smem = functools.partial(pl.BlockSpec, memory_space=pltpu.SMEM)
    half = width // HALVES
    cols = pltpu.VMEM((col_span, width, block), BF16)
    rows = pltpu.VMEM((row_span, width, block), BF16)
    col_half = pltpu.VMEM((col_span, half, block), BF16)
    row_half = pltpu.VMEM((row_span, half, block), BF16)
    arrivals = pltpu.VMEM((row_span + per, width, block), BF16)
    dma = pltpu.SemaphoreType.DMA
    shape = jax.ShapeDtypeStruct(subspace.shape, BF16)
    return pl.pallas_call(
        functools.partial(kernel, n_row, n_col, per, block, width, slots, turned),
        out_shape=(shape, shape),
        in_specs=[smem(), smem(), smem(), smem(), vmem(), pl.BlockSpec(memory_space=pl.ANY)],
        out_specs=(vmem(), vmem()),
        scratch_shapes=[
            pltpu.VMEM((slots, block, block), BF16),
            pltpu.VMEM((slots if turned else 1, block, block), BF16),
            pltpu.VMEM((slots + 1, width, block), F32),
            col_half, col_half, col_half, col_half,
            row_half, row_half, row_half, row_half,
            rows,
            arrivals, arrivals,
            cols, cols, cols,
            pltpu.VMEM((per, half, block), F32),
            pltpu.VMEM((per, width, block), F32),
            pltpu.VMEM((width, block), F32),
            pltpu.SMEM((slots,), jnp.int32),
            pltpu.SMEM((2 * slots,), jnp.int32),
            pltpu.SMEM((row_span * col_span,), jnp.int32),
            pltpu.SMEM((row_span * col_span,), jnp.int32),
            dma((slots,)),
            dma((2, 2, n_col * HALVES)),
            dma((2, n_col * HALVES)),
            dma((2, n_row * HALVES)),
            dma((2, n_row * HALVES)),
            dma((2, n_col * HALVES)),
            dma((2, (n_col + 1) * HALVES)),
            dma((2, n_row * HALVES)),
            dma((2, n_row * HALVES)),
        ],
        compiler_params=pltpu.CompilerParams(
            collective_id=0, has_side_effects=True, vmem_limit_bytes=60 * 1024 * 1024
        ),
    )(tile_blocks, tile_count, cut_bound, top_bound, subspace, hamiltonian)


def solution(mesh):
    return jax.shard_map(
        body,
        mesh=mesh,
        in_specs=(
            P(("temp", "row", "col"), None),
            P(("temp", "row", "col"), None, None),
            P(("row", "col"), None, None),
            P(("row", "col")),
            P("temp"),
            P("temp"),
        ),
        out_specs=(P(("temp", "row", "col"), None), P(("temp", "row", "col"), None)),
        check_vma=False,
    )
```

```python
import functools

import jax
import jax.numpy as jnp
from jax import lax
from jax.experimental import pallas as pl
from jax.experimental.pallas import tpu as pltpu
from jax.sharding import PartitionSpec as P

MESH = pl.DeviceIdType.MESH
F32 = jnp.float32
BF16 = jnp.bfloat16
PIECE = 32
UNROLL = 8
HALVES = 2


def kernel(
    n_row, n_col, per, block, width, slots, turned,
    pairs, count, cut, top, v_ref, t_hbm, out1, out2,
    tbuf, tbuf_t, prod, col00, col01, col10, col11, row00, row01, row10, row11, rb, rsr0, rsr1, cb, crecv0, crecv1, acc, held32, wide,
    keys, vec_slot, row_slot, col_slot, tsem, ag_s, ag_r, xv_s, xv_r, rs_s, rs_r, xc_s, xc_r,
):
    temp = lax.axis_index("temp")
    p = lax.axis_index("row")
    q = lax.axis_index("col")
    row_span = per * n_col
    col_span = per * n_row
    colset = ((col00, col01), (col10, col11))
    rowset = ((row00, row01), (row10, row11))
    half = width // HALVES
    parts = range(HALVES)

    def span(owner):
        return pl.ds(owner * per, per)

    def lines(h):
        return pl.ds(h * half, half)

    rsr = (rsr0, rsr1)
    crecv = (crecv0, crecv1)
    core = lax.rem(p, 2)
    chip = p // 2
    sib = p + 1 - 2 * core
    chips = n_row // 2
    has_left = q > 0
    has_right = q < n_col - 1

    def tile_copy(t):
        return pltpu.make_async_copy(t_hbm.at[t], tbuf.at[t], tsem.at[t])

    def start_tile(t, carry):
        tile_copy(t).start()
        return carry

    lax.fori_loop(0, slots, start_tile, 0)

    barrier = pltpu.get_barrier_semaphore()
    for s in range(n_row):
        @pl.when(s != p)
        def _():
            pl.semaphore_signal(barrier, inc=1, device_id=(temp, s, q), device_id_type=MESH)

    @pl.when(has_left)
    def _():
        pl.semaphore_signal(barrier, inc=1, device_id=(temp, p, q - 1), device_id_type=MESH)

    @pl.when(has_right)
    def _():
        pl.semaphore_signal(barrier, inc=1, device_id=(temp, p, q + 1), device_id_type=MESH)

    pl.semaphore_wait(barrier, n_row - 1 + has_left.astype(jnp.int32) + has_right.astype(jnp.int32))

    center = (cut[0] + top[0]) * 0.5
    half_width = (top[0] - cut[0]) * 0.5

    def ag_copy(a, direction, owner, h, to):
        ref = rowset[a][h].at[span(owner)]
        return pltpu.make_async_remote_copy(
            src_ref=ref, dst_ref=ref,
            send_sem=ag_s.at[a, direction, owner * HALVES + h],
            recv_sem=ag_r.at[a, owner * HALVES + h],
            device_id=(temp, p, to), device_id_type=MESH,
        )

    def xv_copy(a, owner, to, h, send):
        ref = colset[a][h].at[span(owner)]
        return pltpu.make_async_remote_copy(
            src_ref=ref, dst_ref=ref,
            send_sem=xv_s.at[a, send * HALVES + h], recv_sem=xv_r.at[a, owner * HALVES + h],
            device_id=(temp, to, q), device_id_type=MESH,
        )

    def rs_copy(a, d, h, slot, to):
        return pltpu.make_async_remote_copy(
            src_ref=rb.at[span(d), lines(h)], dst_ref=rsr[a].at[span(slot), lines(h)],
            send_sem=rs_s.at[a, d * HALVES + h], recv_sem=rs_r.at[a, slot * HALVES + h],
            device_id=(temp, p, to), device_id_type=MESH,
        )

    def xc_copy(a, d, h, source, to):
        return pltpu.make_async_remote_copy(
            src_ref=cb.at[span(d), lines(h)], dst_ref=crecv[a].at[span(source), lines(h)],
            send_sem=xc_s.at[a, d * HALVES + h], recv_sem=xc_r.at[a, source * HALVES + h],
            device_id=(temp, to, q), device_id_type=MESH,
        )

    def ag_step(a, k, h):
        low = q - k
        high = q + k

        @pl.when(low >= 0)
        def _():
            if k > 0:
                ag_copy(a, 0, low, h, q).wait_recv()
            if k < n_col - 1:
                @pl.when(has_right)
                def _():
                    ag_copy(a, 0, low, h, q + 1).start()

        @pl.when(high < n_col)
        def _():
            if k > 0:
                ag_copy(a, 1, high, h, q).wait_recv()
            if k < n_col - 1:
                @pl.when(has_left)
                def _():
                    ag_copy(a, 1, high, h, q - 1).start()

    def later_chips(fn):
        for x in range(1, chips):
            @pl.when(x > chip)
            def _():
                fn(x)

    def earlier_chips(fn):
        for x in range(chips - 1):
            @pl.when(x < chip)
            def _():
                fn(x)

    def send_vectors(a, h, value):
        colset[a][h][span(p)] = value
        earlier_chips(lambda x: xv_copy(a, p, 2 * x + core, h, 2 * x + core).start())

        @pl.when(core == 1)
        def _():
            xv_copy(a, p, sib, h, sib).start()

        rowset[a][h][span(q)] = value
        ag_step(a, 0, h)

    def forward_copy(a, x, h):
        return xv_copy(a, 2 * x + core, sib, h, 2 * x + core)

    def finish_row_gather(a, h):
        def relay(x):
            forward_copy(a, x, h).wait_recv()
            forward_copy(a, x, h).start()

        later_chips(relay)

        @pl.when(core == 0)
        def _():
            xv_copy(a, sib, sib, h, sib).wait_recv()

        later_chips(lambda x: xv_copy(a, 2 * x + 1 - core, sib, h, sib).wait_recv())

    def find_slots():
        for t in range(slots):
            first = pairs[0, t, 0]
            second = pairs[0, t, 1]
            local_row = first - p * row_span
            local_col = second // row_span * per + lax.rem(second, per)
            vec_slot[t] = jnp.clip(local_col, 0, col_span - 1)
            vec_slot[slots + t] = jnp.clip(local_row, 0, row_span - 1)
            keys[t] = jnp.where(t < count[0], local_row * col_span + local_col, -1)
        held = [keys[t] for t in range(slots)]

        def find(i, carry):
            slot = jnp.int32(slots)
            for t in range(slots):
                slot = jnp.where(held[t] == i, t, slot)
            row_slot[i] = slot
            col_slot[i] = slot
            return carry

        lax.fori_loop(0, row_span * col_span, find, 0)
        for k in range(per):
            col_slot[(q * per + k) * col_span + p * per + k] = slots

    def grouped(lo, hi, one):
        group = UNROLL if (hi - lo) % UNROLL == 0 else 1

        def several(g, carry):
            for u in range(group):
                one(lo + g * group + u)
            return carry

        lax.fori_loop(0, (hi - lo) // group, several, 0)

    def transpose_tiles():
        def one(t, carry):
            tile_copy(t).wait()
            if turned:
                tbuf_t[t] = tbuf[t].T
            return carry

        lax.fori_loop(0, slots, one, 0)

    def row_products(a, h):
        def one(t):
            vectors = colset[a][h][vec_slot[t]]
            if turned:
                prod[t, lines(h), :] = jnp.dot(vectors, tbuf_t[t], preferred_element_type=F32)
            else:
                prod[t, lines(h), :] = lax.dot_general(
                    vectors, tbuf[t], (((1,), (1,)), ((), ())), preferred_element_type=F32
                )

        grouped(0, slots, one)

    def row_totals(h):
        def total(i, carry):
            ids = [row_slot[i * col_span + c] for c in range(col_span)]
            for m in range(half // PIECE):
                rows = pl.ds(h * half + m * PIECE, PIECE)
                acc = prod[ids[0], rows, :]
                for c in range(1, col_span):
                    acc = acc + prod[ids[c], rows, :]
                rb[i, rows, :] = acc.astype(BF16)
            return carry

        lax.fori_loop(0, row_span, total, 0)

    def col_products(a, h):
        def one(t):
            prod[t, lines(h), :] = jnp.dot(
                rowset[a][h][vec_slot[slots + t]], tbuf[t], preferred_element_type=F32
            )

        grouped(0, slots, one)

    def col_totals(h):
        def total(c, carry):
            ids = [col_slot[r * col_span + c] for r in range(row_span)]
            for m in range(half // PIECE):
                rows = pl.ds(h * half + m * PIECE, PIECE)
                acc = prod[ids[0], rows, :]
                for r in range(1, row_span):
                    acc = acc + prod[ids[r], rows, :]
                cb[c, rows, :] = acc.astype(BF16)
            return carry

        lax.fori_loop(p * per, col_span, total, 0)

    def send_to_sibling(a, h):
        @pl.when(core == 0)
        def _():
            xc_copy(a, sib, h, chip, sib).start()

        def to_sibling(x):
            d = 2 * x + 1 - core
            xc_copy(a, d, h, d, sib).start()

        later_chips(to_sibling)

    def send_across(a, h):
        def across(x):
            d = 2 * x + core
            xc_copy(a, d, h, d, sib).wait_recv()
            mine = cb[span(d), lines(h), :].astype(F32)
            cb[span(d), lines(h), :] = (mine + crecv[a][span(d), lines(h), :].astype(F32)).astype(BF16)
            xc_copy(a, d, h, chip, d).start()

        later_chips(across)

    def add_arrival(a, d, h, slot):
        rs_copy(a, d, h, slot, q).wait_recv()
        mine = rb[span(d), lines(h), :].astype(F32)
        rb[span(d), lines(h), :] = (mine + rsr[a][span(slot), lines(h), :].astype(F32)).astype(BF16)

    def rs_step(a, tau, h):
        @pl.when(jnp.logical_and(has_right, tau >= q))
        def _():
            d = n_col - 1 - tau + q

            @pl.when(has_left)
            def _():
                add_arrival(a, d, h, d + 1)

            rs_copy(a, d, h, d + 1, q + 1).start()

        @pl.when(jnp.logical_and(has_left, tau >= n_col - 1 - q))
        def _():
            d = tau - (n_col - 1 - q)

            @pl.when(has_right)
            def _():
                add_arrival(a, d, h, d)

            rs_copy(a, d, h, d, q - 1).start()

    def wait_rs_sends(a):
        for d in range(n_col):
            @pl.when(d != q)
            def _():
                for h in parts:
                    rs_copy(a, d, h, d, q).wait_send()

    def wait_xc_sends(a):
        for s in range(1, n_row):
            @pl.when(s > p)
            def _():
                for h in parts:
                    xc_copy(a, s, h, p, s).wait_send()

    def wait_vector_sends(a):
        for h in parts:
            earlier_chips(lambda x: xv_copy(a, p, 2 * x + core, h, 2 * x + core).wait_send())

            @pl.when(core == 1)
            def _():
                xv_copy(a, p, sib, h, sib).wait_send()

            later_chips(lambda x: forward_copy(a, x, h).wait_send())
            for b in range(n_col):
                @pl.when(jnp.logical_and(has_right, b <= q))
                def _():
                    ag_copy(a, 0, b, h, q).wait_send()

                @pl.when(jnp.logical_and(has_left, b >= q))
                def _():
                    ag_copy(a, 1, b, h, q).wait_send()

    def image(a, h):
        acc[...] = cb[span(p), lines(h), :].astype(F32) + rb[span(q), lines(h), :].astype(F32)

        def add(x):
            xc_copy(a, p, h, x, p).wait_recv()
            acc[...] += crecv[a][span(x), lines(h), :].astype(F32)

        @pl.when(core == 1)
        def _():
            add(chip)

        earlier_chips(add)

        @pl.when(has_left)
        def _():
            rs_copy(a, q, h, q + 1, q).wait_recv()
            acc[...] += rsr[a][span(q + 1), lines(h), :].astype(F32)

        @pl.when(has_right)
        def _():
            rs_copy(a, q, h, q, q).wait_recv()
            acc[...] += rsr[a][span(q), lines(h), :].astype(F32)

        return acc[...]

    def apply(a):
        if a == 0:
            transpose_tiles()
        else:
            wait_rs_sends(a - 1)
        for h in parts:
            finish_row_gather(a, h)
            ag_step(a, 1, h)
            row_products(a, h)
            row_totals(h)
            rs_step(a, 0, h)
        for h in parts:
            for k in range(2, n_col - 1):
                ag_step(a, k, h)
            rs_step(a, 1, h)
        if a > 0:
            wait_xc_sends(a - 1)
        for h in parts:
            ag_step(a, n_col - 1, h)
            col_products(a, h)
            col_totals(h)
            send_to_sibling(a, h)
            rs_step(a, 2, h)
            send_across(a, h)

        def step(tau, carry):
            for h in parts:
                rs_step(a, tau, h)
            return carry

        lax.fori_loop(3, n_col - 1, step, 0)

    prod[slots] = jnp.zeros((width, block), F32)
    for k in range(per):
        held32[k] = v_ref[k * block:(k + 1) * block, :].astype(F32).T
    for h in parts:
        send_vectors(0, h, held32[:, lines(h), :].astype(BF16))
    find_slots()
    apply(0)
    for h in parts:
        vectors = held32[:, lines(h), :]
        send_vectors(1, h, ((image(0, h) - center * vectors) / half_width).astype(BF16))
    for k in range(per):
        for h in parts:
            wide[lines(h), :] = colset[1][h][p * per + k].astype(F32)
        out1[k * block:(k + 1) * block, :] = wide[...].T.astype(BF16)
    apply(1)
    for h in parts:
        first = colset[1][h][span(p)].astype(F32)
        vectors = held32[:, lines(h), :]
        held32[:, lines(h), :] = 2.0 * (image(1, h) - center * first) / half_width - vectors
    for k in range(per):
        out2[k * block:(k + 1) * block, :] = held32[k].T.astype(BF16)
    wait_rs_sends(1)
    wait_xc_sends(1)
    wait_vector_sends(0)
    wait_vector_sends(1)


def body(subspace, hamiltonian, tile_blocks, tile_count, cut_bound, top_bound):
    block = hamiltonian.shape[1]
    width = subspace.shape[1]
    slots = hamiltonian.shape[0]
    per = subspace.shape[0] // block
    n_row = lax.axis_size("row")
    n_col = lax.axis_size("col")
    row_span = per * n_col
    col_span = per * n_row
    turned = row_span + col_span <= slots
    vmem = functools.partial(pl.BlockSpec, memory_space=pltpu.VMEM)
    smem = functools.partial(pl.BlockSpec, memory_space=pltpu.SMEM)
    half = width // HALVES
    cols = pltpu.VMEM((col_span, width, block), BF16)
    rows = pltpu.VMEM((row_span, width, block), BF16)
    col_half = pltpu.VMEM((col_span, half, block), BF16)
    row_half = pltpu.VMEM((row_span, half, block), BF16)
    arrivals = pltpu.VMEM((row_span + per, width, block), BF16)
    dma = pltpu.SemaphoreType.DMA
    shape = jax.ShapeDtypeStruct(subspace.shape, BF16)
    return pl.pallas_call(
        functools.partial(kernel, n_row, n_col, per, block, width, slots, turned),
        out_shape=(shape, shape),
        in_specs=[smem(), smem(), smem(), smem(), vmem(), pl.BlockSpec(memory_space=pl.ANY)],
        out_specs=(vmem(), vmem()),
        scratch_shapes=[
            pltpu.VMEM((slots, block, block), BF16),
            pltpu.VMEM((slots if turned else 1, block, block), BF16),
            pltpu.VMEM((slots + 1, width, block), F32),
            col_half, col_half, col_half, col_half,
            row_half, row_half, row_half, row_half,
            rows,
            arrivals, arrivals,
            cols, cols, cols,
            pltpu.VMEM((per, half, block), F32),
            pltpu.VMEM((per, width, block), F32),
            pltpu.VMEM((width, block), F32),
            pltpu.SMEM((slots,), jnp.int32),
            pltpu.SMEM((2 * slots,), jnp.int32),
            pltpu.SMEM((row_span * col_span,), jnp.int32),
            pltpu.SMEM((row_span * col_span,), jnp.int32),
            dma((slots,)),
            dma((2, 2, n_col * HALVES)),
            dma((2, n_col * HALVES)),
            dma((2, n_row * HALVES)),
            dma((2, n_row * HALVES)),
            dma((2, n_col * HALVES)),
            dma((2, (n_col + 1) * HALVES)),
            dma((2, n_row * HALVES)),
            dma((2, n_row * HALVES)),
        ],
        compiler_params=pltpu.CompilerParams(
            collective_id=0, has_side_effects=True, vmem_limit_bytes=60 * 1024 * 1024
        ),
    )(tile_blocks, tile_count, cut_bound, top_bound, subspace, hamiltonian)


def solution(mesh):
    return jax.shard_map(
        body,
        mesh=mesh,
        in_specs=(
            P(("temp", "row", "col"), None),
            P(("temp", "row", "col"), None, None),
            P(("row", "col"), None, None),
            P(("row", "col")),
            P("temp"),
            P("temp"),
        ),
        out_specs=(P(("temp", "row", "col"), None), P(("temp", "row", "col"), None)),
        check_vma=False,
    )
```
